32 devices in a mesh: parts: 2 (over y), shard: 2 (over core), blk: 8 (over z, x).
Axes of the slice: x: 2, y: 2, z: 4, core: 2. Of those that a mesh axis runs over, the one named last changes fastest.
Arguments:
- queries_in: bfloat16 [4096, 1024], P(('parts', 'shard', 'blk')), parts along dimension 0, may hold values from -12 to 12
- query_weight: bfloat16 [1024, 1024], replicated, may hold values from -0.1875 to 0.1875
- bank: bfloat16 [2048, 1024], P(('parts', 'shard', 'blk')), parts along dimension 0, may hold values from -110 to 110
- uses: int32 [4096, 2], P(('parts', 'shard', 'blk')), parts along dimension 0, may hold values from 0 to 1, as said below
Outputs:
- retrieved: bfloat16 [4096, 1024], P(('parts', 'shard', 'blk')), parts along dimension 0
The draws below stay inside these ranges and needn't reach their ends.
There are 2 independent parts, one for each index of `parts`. The reference program is written for one: setup_inputs(seed, part) draws one part's arguments, and reference() takes and returns one part's arrays. A program takes and returns all parts, laid end to end along the dimension named above; an argument that names none is the same for every part. Nothing has to cross between parts.
Inputs may be any that keep to these rules, and one draw needn't show every extreme that they name: `uses`: every query lists one or both of the two shards. Of the 128 queries of one device, at most 128 list one shard, and in every draw for every index of blk the queries of both devices at that index all list one same shard.
All inputs are finite; a program needn't handle non-finite values.
Results may differ from the reference program's by a relative error of at most 0.035.
Values may be sent and summed in bfloat16 or wider, within the bound.
A program may use at most 128 MiB of HBM per device.

```python
import jax
import jax.numpy as jnp
from jax import lax

HEADS = 8
HEAD_DIM = 128
D = 1024
Q_DEV = 128
QUERIES = 2048
BANK = 1024
BANK_SHARD = 512


def draw_bank(key, part):
    key_base = jax.random.fold_in(key, 0)
    return jax.random.normal(key_base, (BANK, D), jnp.float32).astype(jnp.bfloat16)


def draw_uses(key, part):
    blocks = QUERIES // Q_DEV
    columns = blocks // 2
    key_hot, key_count, key_order = jax.random.split(key, 3)
    hottest = jax.random.randint(key_hot, (columns,), 0, 2)
    hottest = jnp.concatenate([hottest, hottest])
    lowest = max(1, Q_DEV // 8)
    highest = Q_DEV // 2 + 1
    cold_count = jax.random.randint(key_count, (blocks,), lowest, highest)
    ranking = jax.vmap(lambda member: jax.random.permutation(member, Q_DEV))(jax.random.split(key_order, blocks))
    cold = (ranking < cold_count[:, None]).astype(jnp.int32)
    first = jnp.where(hottest[:, None] == 0, 1, cold)
    second = jnp.where(hottest[:, None] == 1, 1, cold)
    return jnp.stack([first, second], -1).reshape(QUERIES, 2).astype(jnp.int32)


def levels(rng, shape, pieces, smallest, high):
    gain, own = 1.0, jax.random.fold_in(rng, 6)
    for dim, shards_of in pieces:
        draws = jnp.exp(jax.random.uniform(jax.random.fold_in(own, dim), (shards_of,), jnp.float32, smallest / len(pieces), high / len(pieces)))
        gain = gain * jnp.repeat(draws, shape[dim] // shards_of).reshape([-1 if axis == dim else 1 for axis in range(len(shape))])
    return gain


def noise(own_key, shape, width, limit, pieces=(), dtype=jnp.bfloat16):
    factor_of = levels(own_key, shape, pieces, -0.22, 0.18) if pieces else 1.0
    drawn = jax.random.normal(own_key, shape, jnp.float32) * width * factor_of
    return jnp.minimum(jnp.maximum(drawn, -limit), limit).astype(dtype)


def setup_inputs(seed: int = 0, part: int = 0) -> dict:
    arg_keys = jax.random.split(jax.random.key(seed), 5)
    own_keys = jax.random.split(jax.random.fold_in(arg_keys[4], part), 5)
    queries_in = noise(own_keys[0], (QUERIES, D), 2.0, 12.0, ((0, 16),))
    query_weight = noise(arg_keys[1], (D, D), D ** -0.5, 0.1875)
    bank = draw_bank(jax.random.fold_in(jax.random.fold_in(arg_keys[4], part), 71), part)
    uses = draw_uses(jax.random.fold_in(jax.random.fold_in(arg_keys[4], part), 71), part)
    return {"queries_in": queries_in, "query_weight": query_weight, "bank": bank, "uses": uses}


NEGATIVE = -1e30


def reference(queries_in, query_weight, bank, uses):
    projected = jnp.dot(queries_in, query_weight, preferred_element_type=jnp.float32).astype(jnp.bfloat16)
    keys_all = bank.astype(jnp.float32).reshape(BANK, HEADS, HEAD_DIM)
    shard_of = (jnp.arange(BANK) // BANK_SHARD).astype(jnp.int32)
    logit_scale = HEAD_DIM ** -0.5

    def attend(inputs):
        query_block, uses_block = inputs
        query_heads = query_block.astype(jnp.float32).reshape(Q_DEV, HEADS, HEAD_DIM)
        scores = jnp.einsum("thd,rhd->thr", query_heads, keys_all) * logit_scale
        allowed = jnp.where(shard_of[None, :] == 0, uses_block[:, 0:1], uses_block[:, 1:2]) > 0
        scores = jnp.where(allowed[:, None, :], scores, NEGATIVE)
        highest = jnp.max(scores, axis=-1, keepdims=True)
        weights = jnp.where(allowed[:, None, :], jnp.exp(scores - highest), 0.0)
        total = jnp.sum(weights, axis=-1)
        rounded = lax.optimization_barrier(weights.astype(jnp.bfloat16)).astype(jnp.float32)
        summed = jnp.einsum("thr,rhd->thd", rounded, keys_all)
        return (summed / total[..., None]).reshape(Q_DEV, HEADS * HEAD_DIM).astype(jnp.bfloat16)

    retrieved = lax.map(attend, (projected.reshape(-1, Q_DEV, HEADS * HEAD_DIM), uses.reshape(-1, Q_DEV, 2)))
    return retrieved.reshape(-1, HEADS * HEAD_DIM)
```

```python
import math

import jax
import jax.numpy as jnp
from jax import lax
from jax.sharding import PartitionSpec as P

HEADS = 8
HEAD_DIM = 128
NEGATIVE = -1e30


def local_xla(queries_in, query_weight, bank, uses):
    rows = queries_in.shape[0]
    projected = jnp.dot(queries_in, query_weight, preferred_element_type=jnp.float32).astype(
        jnp.bfloat16
    )
    heads = projected.reshape(rows, HEADS, HEAD_DIM)
    whole = lax.all_gather(bank, ("shard", "blk"), axis=0, tiled=True)
    shard_rows = whole.shape[0] // 2
    chunk_rows = math.gcd(shard_rows, 512)
    chunks = shard_rows // chunk_rows
    blocked = whole.reshape(2, chunks, chunk_rows, HEADS, HEAD_DIM)
    allowed = uses > 0

    def step(carry, keys):
        top_old, total_old, accum_old = carry
        scores = jnp.einsum("thd,srhd->htsr", heads, keys, preferred_element_type=jnp.float32)
        scores = jnp.where(allowed[None, :, :, None], scores * HEAD_DIM**-0.5, NEGATIVE)
        top = jnp.maximum(top_old, jnp.max(scores, axis=(2, 3)))
        weights = jnp.exp(scores - top[:, :, None, None])
        factor = jnp.exp(top_old - top)
        total = total_old * factor + jnp.sum(weights, axis=(2, 3))
        accum = accum_old * factor[..., None] + jnp.einsum(
            "htsr,srhd->htd",
            weights.astype(jnp.bfloat16),
            keys,
            preferred_element_type=jnp.float32,
        )
        return (top, total, accum), None

    start = (
        jnp.full((HEADS, rows), NEGATIVE, jnp.float32),
        jnp.zeros((HEADS, rows), jnp.float32),
        jnp.zeros((HEADS, rows, HEAD_DIM), jnp.float32),
    )
    (top, total, accum), _ = lax.scan(step, start, blocked.transpose(1, 0, 2, 3, 4))
    out = (accum / total[..., None]).astype(jnp.bfloat16)
    return out.transpose(1, 0, 2).reshape(rows, HEADS * HEAD_DIM)


def solution(mesh):
    spec = P(("parts", "shard", "blk"), None)
    return jax.shard_map(
        local_xla, mesh=mesh, in_specs=(spec, P(), spec, spec), out_specs=spec, check_vma=False
    )
```

```python
import functools
import math

import jax
import jax.numpy as jnp
from jax import lax
from jax.experimental import pallas as pl
from jax.experimental.pallas import tpu as pltpu
from jax.sharding import PartitionSpec as P

HEADS = 8
HEAD_DIM = 128
NEGATIVE = -1e30
ALONG_X = 2
MESH = pl.DeviceIdType.MESH


def kernel(
    depth,
    queries_hbm,
    weight_hbm,
    bank_hbm,
    uses_ref,
    out_ref,
    held,
    queries_ref,
    weight_ref,
    projected,
    top_ref,
    total_ref,
    accum_ref,
    load_sems,
    z_sems,
    x_sems,
    core_sems,
    recv_sems,
):
    part = lax.axis_index("parts")
    core = lax.axis_index("shard")
    blk = lax.axis_index("blk")
    z, x = blk // ALONG_X, blk % ALONG_X
    other_x, other_core = 1 - x, 1 - core

    def at(to_core, to_z, to_x):
        return (part, to_core, to_z * ALONG_X + to_x)

    def copy(of_z, of_core, of_x, sems, target, source=None):
        slot = held.at[of_z, of_core, of_x]
        return pltpu.make_async_remote_copy(
            src_ref=slot if source is None else source,
            dst_ref=slot,
            send_sem=sems.at[of_z, of_x],
            recv_sem=recv_sems.at[of_z, of_core, of_x],
            device_id=target,
            device_id_type=MESH,
        )

    def along(of_z, step, source=None):
        return copy(of_z, core, x, z_sems.at[0 if step > 0 else 1], at(core, z + step, x), source)

    def across(of_z, source=None):
        return copy(of_z, core, x, x_sems, at(core, z, other_x), source)

    def over(of_z, of_x, source=None):
        return copy(of_z, core, of_x, core_sems, at(other_core, z, x), source)

    def arrived(of_z, of_core, of_x):
        copy(of_z, of_core, of_x, x_sems, at(core, z, other_x)).wait_recv()

    loads = [
        pltpu.make_async_copy(weight_hbm, weight_ref, load_sems.at[0]),
        pltpu.make_async_copy(queries_hbm, queries_ref, load_sems.at[1]),
        pltpu.make_async_copy(bank_hbm, held.at[z, core, x], load_sems.at[2]),
    ]
    for load in loads:
        load.start()

    barrier = pltpu.get_barrier_semaphore()
    below, above = z > 0, z < depth - 1

    def greet(target):
        pl.semaphore_signal(barrier, inc=1, device_id=target, device_id_type=MESH)

    greet(at(core, z, other_x))
    greet(at(other_core, z, x))
    pl.when(below)(lambda: greet(at(core, z - 1, x)))
    pl.when(above)(lambda: greet(at(core, z + 1, x)))
    pl.semaphore_wait(barrier, 2 + below.astype(jnp.int32) + above.astype(jnp.int32))

    pl.when(below)(lambda: along(z, -1, bank_hbm).start())
    pl.when(above)(lambda: along(z, 1, bank_hbm).start())
    across(z, bank_hbm).start()
    over(z, x, bank_hbm).start()

    for load in loads[:2]:
        load.wait()
    for head in range(0, HEADS, 2):
        columns = slice(head * HEAD_DIM, (head + 2) * HEAD_DIM)
        projected[:, columns] = jnp.dot(
            queries_ref[...], weight_ref[:, columns], preferred_element_type=jnp.float32
        ).astype(jnp.bfloat16)
    loads[2].wait()

    factor = HEAD_DIM**-0.5 * math.log2(math.e)
    rows = held.shape[3]
    plane_rows = 2 * ALONG_X * rows
    rows_q = projected.shape[0]

    def attend(of_z, first):
        in_second = (
            lax.broadcasted_iota(jnp.int32, (rows_q, plane_rows), 1) >= ALONG_X * rows
        )
        allowed = jnp.where(in_second, uses_ref[:, 1:2], uses_ref[:, 0:1]) > 0
        for head in range(HEADS):
            columns = slice(head * HEAD_DIM, (head + 1) * HEAD_DIM)
            keys = held[of_z, :, :, :, columns].reshape(plane_rows, HEAD_DIM)
            scores = lax.dot_general(
                projected[:, columns],
                keys,
                (((1,), (1,)), ((), ())),
                preferred_element_type=jnp.float32,
            )
            scores = jnp.where(allowed, scores * factor, NEGATIVE)
            top = jnp.max(scores, axis=1, keepdims=True)
            if not first:
                top_old = top_ref[head]
                top = jnp.maximum(top_old, top)
            weights = jnp.exp2(scores - top[:, :1])
            total = weights[:, :HEAD_DIM]
            for start in range(HEAD_DIM, plane_rows, HEAD_DIM):
                total = total + weights[:, start : start + HEAD_DIM]
            summed = jnp.dot(
                weights.astype(jnp.bfloat16), keys, preferred_element_type=jnp.float32
            )
            if first:
                top = jnp.broadcast_to(top, (rows_q, HEAD_DIM))
            else:
                shrink = jnp.exp2(top_old - top)
                total = total + total_ref[head] * shrink
                summed = summed + accum_ref[head] * shrink
            top_ref[head] = top
            total_ref[head] = total
            accum_ref[head] = summed

    def planes(distance, action):
        if distance == 0:
            action(z, 0)
            return
        pl.when(z >= distance)(lambda: action(z - distance, 1))
        pl.when(z < depth - distance)(lambda: action(z + distance, -1))

    def relay(of_z, step):
        arrived(of_z, core, x)
        pl.when((z + step >= 0) & (z + step < depth))(lambda: along(of_z, step).start())
        across(of_z).start()
        over(of_z, x).start()

    def hand_over(of_z, step):
        arrived(of_z, core, other_x)
        over(of_z, other_x).start()

    def finish_plane(of_z, step):
        arrived(of_z, other_core, 0)
        arrived(of_z, other_core, 1)
        attend(of_z, step == 0)

    for distance in range(depth):
        if distance + 1 < depth:
            planes(distance + 1, relay)
        planes(distance, hand_over)
        planes(distance, finish_plane)

    for head in range(HEADS):
        columns = slice(head * HEAD_DIM, (head + 1) * HEAD_DIM)
        total = jnp.sum(total_ref[head], axis=1, keepdims=True)
        out_ref[:, columns] = (accum_ref[head] / total).astype(out_ref.dtype)

    for of_z in range(depth):
        pl.when((z >= of_z) & above)(lambda of_z=of_z: along(of_z, 1).wait_send())
        pl.when((z <= of_z) & below)(lambda of_z=of_z: along(of_z, -1).wait_send())
        across(of_z).wait_send()
        for of_x in range(ALONG_X):
            over(of_z, of_x).wait_send()


def local_kernel(depth, queries_in, query_weight, bank, uses):
    rows_q, width = queries_in.shape
    rows = bank.shape[0]
    any_space = pl.BlockSpec(memory_space=pl.ANY)
    return pl.pallas_call(
        functools.partial(kernel, depth),
        out_shape=jax.ShapeDtypeStruct((rows_q, HEADS * HEAD_DIM), jnp.bfloat16),
        in_specs=[any_space, any_space, any_space, pl.BlockSpec(memory_space=pltpu.VMEM)],
        out_specs=pl.BlockSpec(memory_space=pltpu.VMEM),
        scratch_shapes=[
            pltpu.VMEM((depth, 2, ALONG_X, rows, width), jnp.bfloat16),
            pltpu.VMEM((rows_q, width), jnp.bfloat16),
            pltpu.VMEM((width, width), jnp.bfloat16),
            pltpu.VMEM((rows_q, width), jnp.bfloat16),
            pltpu.VMEM((HEADS, rows_q, HEAD_DIM), jnp.float32),
            pltpu.VMEM((HEADS, rows_q, HEAD_DIM), jnp.float32),
            pltpu.VMEM((HEADS, rows_q, HEAD_DIM), jnp.float32),
            pltpu.SemaphoreType.DMA((3,)),
            pltpu.SemaphoreType.DMA((2, depth, ALONG_X)),
            pltpu.SemaphoreType.DMA((depth, ALONG_X)),
            pltpu.SemaphoreType.DMA((depth, ALONG_X)),
            pltpu.SemaphoreType.DMA((depth, 2, ALONG_X)),
        ],
        compiler_params=pltpu.CompilerParams(
            collective_id=0, has_side_effects=True, vmem_limit_bytes=32 * 2**20
        ),
        name="gather_attend",
    )(queries_in, query_weight, bank, uses)


def local_xla(queries_in, query_weight, bank, uses):
    rows = queries_in.shape[0]
    projected = jnp.dot(queries_in, query_weight, preferred_element_type=jnp.float32).astype(
        jnp.bfloat16
    )
    heads = projected.reshape(rows, HEADS, HEAD_DIM)
    whole = lax.all_gather(bank, ("shard", "blk"), axis=0, tiled=True)
    shard_rows = whole.shape[0] // 2
    chunk_rows = math.gcd(shard_rows, 512)
    chunks = shard_rows // chunk_rows
    blocked = whole.reshape(2, chunks, chunk_rows, HEADS, HEAD_DIM)
    allowed = uses > 0

    def step(carry, keys):
        top_old, total_old, accum_old = carry
        scores = jnp.einsum("thd,srhd->htsr", heads, keys, preferred_element_type=jnp.float32)
        scores = jnp.where(allowed[None, :, :, None], scores * HEAD_DIM**-0.5, NEGATIVE)
        top = jnp.maximum(top_old, jnp.max(scores, axis=(2, 3)))
        weights = jnp.exp(scores - top[:, :, None, None])
        factor = jnp.exp(top_old - top)
        total = total_old * factor + jnp.sum(weights, axis=(2, 3))
        accum = accum_old * factor[..., None] + jnp.einsum(
            "htsr,srhd->htd",
            weights.astype(jnp.bfloat16),
            keys,
            preferred_element_type=jnp.float32,
        )
        return (top, total, accum), None

    start = (
        jnp.full((HEADS, rows), NEGATIVE, jnp.float32),
        jnp.zeros((HEADS, rows), jnp.float32),
        jnp.zeros((HEADS, rows, HEAD_DIM), jnp.float32),
    )
    (top, total, accum), _ = lax.scan(step, start, blocked.transpose(1, 0, 2, 3, 4))
    out = (accum / total[..., None]).astype(jnp.bfloat16)
    return out.transpose(1, 0, 2).reshape(rows, HEADS * HEAD_DIM)


def solution(mesh):
    spec = P(("parts", "shard", "blk"), None)
    blocks = mesh.shape["blk"]
    local = functools.partial(local_kernel, blocks // ALONG_X) if blocks == 8 else local_xla
    return jax.shard_map(
        local, mesh=mesh, in_specs=(spec, P(), spec, spec), out_specs=spec, check_vma=False
    )
```

```python
import functools
import math

import jax
import jax.numpy as jnp
from jax import lax
from jax.experimental import pallas as pl
from jax.experimental.pallas import tpu as pltpu
from jax.sharding import PartitionSpec as P

HEADS = 8
HEAD_DIM = 128
NEGATIVE = -1e30
ALONG_X = 2
PIECES = 2
MESH = pl.DeviceIdType.MESH


def kernel(
    depth,
    queries_hbm,
    weight_hbm,
    bank_hbm,
    uses_ref,
    out_ref,
    held,
    queries_ref,
    weight_ref,
    projected,
    top_ref,
    total_ref,
    accum_ref,
    masks,
    load_sems,
    z_sems,
    x_sems,
    core_sems,
    recv_sems,
):
    part = lax.axis_index("parts")
    core = lax.axis_index("shard")
    blk = lax.axis_index("blk")
    z, x = blk // ALONG_X, blk % ALONG_X
    other_x, other_core = 1 - x, 1 - core

    def at(to_core, to_z, to_x):
        return (part, to_core, to_z * ALONG_X + to_x)

    bank_rows = bank_hbm.shape[0] // PIECES

    def copy(of_z, of_core, of_x, piece, sems, target, own=False):
        slot = held.at[of_z, of_core, of_x, piece]
        return pltpu.make_async_remote_copy(
            src_ref=bank_hbm.at[pl.ds(piece * bank_rows, bank_rows)] if own else slot,
            dst_ref=slot,
            send_sem=sems.at[of_z, of_x, piece],
            recv_sem=recv_sems.at[of_z, of_core, of_x, piece],
            device_id=target,
            device_id_type=MESH,
        )

    def along(of_z, piece, step, own=False):
        sems = z_sems.at[0 if step > 0 else 1]
        return copy(of_z, core, x, piece, sems, at(core, z + step, x), own)

    def across(of_z, piece, own=False):
        return copy(of_z, core, x, piece, x_sems, at(core, z, other_x), own)

    def over(of_z, of_x, piece, own=False):
        return copy(of_z, core, of_x, piece, core_sems, at(other_core, z, x), own)

    def arrived(of_z, of_core, of_x, piece):
        copy(of_z, of_core, of_x, piece, x_sems, at(core, z, other_x)).wait_recv()

    loads = [
        pltpu.make_async_copy(weight_hbm, weight_ref, load_sems.at[0]),
        pltpu.make_async_copy(queries_hbm, queries_ref, load_sems.at[1]),
    ] + [
        pltpu.make_async_copy(
            bank_hbm.at[pl.ds(piece * bank_rows, bank_rows)],
            held.at[z, core, x, piece],
            load_sems.at[2 + piece],
        )
        for piece in range(PIECES)
    ]
    for load in loads:
        load.start()

    barrier = pltpu.get_barrier_semaphore()
    below, above = z > 0, z < depth - 1

    def greet(target):
        pl.semaphore_signal(barrier, inc=1, device_id=target, device_id_type=MESH)

    greet(at(core, z, other_x))
    greet(at(other_core, z, x))
    pl.when(below)(lambda: greet(at(core, z - 1, x)))
    pl.when(above)(lambda: greet(at(core, z + 1, x)))
    pl.semaphore_wait(barrier, 2 + below.astype(jnp.int32) + above.astype(jnp.int32))

    for piece in range(PIECES):
        pl.when(below)(lambda piece=piece: along(z, piece, -1, True).start())
        pl.when(above)(lambda piece=piece: along(z, piece, 1, True).start())
        across(z, piece, True).start()
    for piece in range(PIECES):
        over(z, x, piece, True).start()

    for load in loads[:2]:
        load.wait()
    for head in range(0, HEADS, 2):
        columns = slice(head * HEAD_DIM, (head + 2) * HEAD_DIM)
        projected[:, columns] = jnp.dot(
            queries_ref[...], weight_ref[:, columns], preferred_element_type=jnp.float32
        ).astype(jnp.bfloat16)
    for load in loads[2:]:
        load.wait()
    for shard in range(2):
        listed = uses_ref[shard : shard + 1, :].astype(jnp.float32)
        masks[shard] = jnp.broadcast_to(listed, (HEAD_DIM, listed.shape[1])).T

    factor = HEAD_DIM**-0.5 * math.log2(math.e)
    rows = bank_hbm.shape[0]
    plane_rows = 2 * ALONG_X * rows
    rows_q = projected.shape[0]

    def attend(of_z, first):
        repeats = ALONG_X * rows // HEAD_DIM
        allowed = jnp.concatenate([masks[0]] * repeats + [masks[1]] * repeats, axis=1) > 0.5
        for head in range(HEADS):
            columns = slice(head * HEAD_DIM, (head + 1) * HEAD_DIM)
            keys = held[of_z, :, :, :, :, columns].reshape(plane_rows, HEAD_DIM)
            scores = lax.dot_general(
                projected[:, columns],
                keys,
                (((1,), (1,)), ((), ())),
                preferred_element_type=jnp.float32,
            )
            scores = jnp.where(allowed, scores * factor, NEGATIVE)
            top = jnp.max(scores, axis=1, keepdims=True)
            if not first:
                top_old = top_ref[head]
                top = jnp.maximum(top_old, top)
            weights = jnp.exp2(scores - top[:, :1])
            total = weights[:, :HEAD_DIM]
            for start in range(HEAD_DIM, plane_rows, HEAD_DIM):
                total = total + weights[:, start : start + HEAD_DIM]
            summed = jnp.dot(
                weights.astype(jnp.bfloat16), keys, preferred_element_type=jnp.float32
            )
            if first:
                top = jnp.broadcast_to(top, (rows_q, HEAD_DIM))
            else:
                shrink = jnp.exp2(top_old - top)
                total = total + total_ref[head] * shrink
                summed = summed + accum_ref[head] * shrink
            top_ref[head] = top
            total_ref[head] = total
            accum_ref[head] = summed

    def planes(distance, action):
        if distance == 0:
            action(z, 0)
            return
        pl.when(z >= distance)(lambda: action(z - distance, 1))
        pl.when(z < depth - distance)(lambda: action(z + distance, -1))

    def relay(of_z, step):
        for piece in range(PIECES):
            arrived(of_z, core, x, piece)
            pl.when((z + step >= 0) & (z + step < depth))(
                lambda piece=piece: along(of_z, piece, step).start()
            )
            across(of_z, piece).start()
            over(of_z, x, piece).start()

    def hand_over(of_z, step):
        for piece in range(PIECES):
            arrived(of_z, core, other_x, piece)
            over(of_z, other_x, piece).start()

    def finish_plane(of_z, step):
        for of_x in range(ALONG_X):
            for piece in range(PIECES):
                arrived(of_z, other_core, of_x, piece)
        attend(of_z, step == 0)

    for distance in range(depth):
        if distance + 1 < depth:
            planes(distance + 1, relay)
        planes(distance, hand_over)
        planes(distance, finish_plane)

    for head in range(HEADS):
        columns = slice(head * HEAD_DIM, (head + 1) * HEAD_DIM)
        total = jnp.sum(total_ref[head], axis=1, keepdims=True)
        out_ref[:, columns] = (accum_ref[head] / total).astype(out_ref.dtype)

    def drain(of_z, piece):
        pl.when((z >= of_z) & above)(lambda: along(of_z, piece, 1).wait_send())
        pl.when((z <= of_z) & below)(lambda: along(of_z, piece, -1).wait_send())
        across(of_z, piece).wait_send()
        for of_x in range(ALONG_X):
            over(of_z, of_x, piece).wait_send()

    for of_z in range(depth):
        for piece in range(PIECES):
            drain(of_z, piece)


def local_kernel(depth, queries_in, query_weight, bank, uses):
    rows_q, width = queries_in.shape
    rows = bank.shape[0]
    any_space = pl.BlockSpec(memory_space=pltpu.HBM)
    return pl.pallas_call(
        functools.partial(kernel, depth),
        out_shape=jax.ShapeDtypeStruct((rows_q, HEADS * HEAD_DIM), jnp.bfloat16),
        in_specs=[any_space, any_space, any_space, pl.BlockSpec(memory_space=pltpu.VMEM)],
        out_specs=pl.BlockSpec(memory_space=pltpu.VMEM),
        scratch_shapes=[
            pltpu.VMEM((depth, 2, ALONG_X, PIECES, rows // PIECES, width), jnp.bfloat16),
            pltpu.VMEM((rows_q, width), jnp.bfloat16),
            pltpu.VMEM((width, width), jnp.bfloat16),
            pltpu.VMEM((rows_q, width), jnp.bfloat16),
            pltpu.VMEM((HEADS, rows_q, HEAD_DIM), jnp.float32),
            pltpu.VMEM((HEADS, rows_q, HEAD_DIM), jnp.float32),
            pltpu.VMEM((HEADS, rows_q, HEAD_DIM), jnp.float32),
            pltpu.VMEM((2, rows_q, HEAD_DIM), jnp.float32),
            pltpu.SemaphoreType.DMA((2 + PIECES,)),
            pltpu.SemaphoreType.DMA((2, depth, ALONG_X, PIECES)),
            pltpu.SemaphoreType.DMA((depth, ALONG_X, PIECES)),
            pltpu.SemaphoreType.DMA((depth, ALONG_X, PIECES)),
            pltpu.SemaphoreType.DMA((depth, 2, ALONG_X, PIECES)),
        ],
        compiler_params=pltpu.CompilerParams(
            collective_id=0, has_side_effects=True, vmem_limit_bytes=56 * 2**20
        ),
        name="gather_attend",
    )(queries_in, query_weight, bank, uses.T)


def local_xla(queries_in, query_weight, bank, uses):
    rows = queries_in.shape[0]
    projected = jnp.dot(queries_in, query_weight, preferred_element_type=jnp.float32).astype(
        jnp.bfloat16
    )
    heads = projected.reshape(rows, HEADS, HEAD_DIM)
    whole = lax.all_gather(bank, ("shard", "blk"), axis=0, tiled=True)
    shard_rows = whole.shape[0] // 2
    chunk_rows = math.gcd(shard_rows, 512)
    chunks = shard_rows // chunk_rows
    blocked = whole.reshape(2, chunks, chunk_rows, HEADS, HEAD_DIM)
    allowed = uses > 0

    def step(carry, keys):
        top_old, total_old, accum_old = carry
        scores = jnp.einsum("thd,srhd->htsr", heads, keys, preferred_element_type=jnp.float32)
        scores = jnp.where(allowed[None, :, :, None], scores * HEAD_DIM**-0.5, NEGATIVE)
        top = jnp.maximum(top_old, jnp.max(scores, axis=(2, 3)))
        weights = jnp.exp(scores - top[:, :, None, None])
        factor = jnp.exp(top_old - top)
        total = total_old * factor + jnp.sum(weights, axis=(2, 3))
        accum = accum_old * factor[..., None] + jnp.einsum(
            "htsr,srhd->htd",
            weights.astype(jnp.bfloat16),
            keys,
            preferred_element_type=jnp.float32,
        )
        return (top, total, accum), None

    start = (
        jnp.full((HEADS, rows), NEGATIVE, jnp.float32),
        jnp.zeros((HEADS, rows), jnp.float32),
        jnp.zeros((HEADS, rows, HEAD_DIM), jnp.float32),
    )
    (top, total, accum), _ = lax.scan(step, start, blocked.transpose(1, 0, 2, 3, 4))
    out = (accum / total[..., None]).astype(jnp.bfloat16)
    return out.transpose(1, 0, 2).reshape(rows, HEADS * HEAD_DIM)


def solution(mesh):
    spec = P(("parts", "shard", "blk"), None)
    blocks = mesh.shape["blk"]
    local = functools.partial(local_kernel, blocks // ALONG_X) if blocks == 8 else local_xla
    return jax.shard_map(
        local, mesh=mesh, in_specs=(spec, P(), spec, spec), out_specs=spec, check_vma=False
    )
```

```python
import functools
import math

import jax
import jax.numpy as jnp
from jax import lax
from jax.experimental import pallas as pl
from jax.experimental.pallas import tpu as pltpu
from jax.sharding import PartitionSpec as P

HEADS = 8
HEAD_DIM = 128
NEGATIVE = -1e30
ALONG_X = 2
PIECES = 2
MESH = pl.DeviceIdType.MESH


def kernel(
    depth,
    queries_hbm,
    weight_hbm,
    bank_hbm,
    uses_ref,
    out_ref,
    held,
    queries_ref,
    weight_ref,
    projected,
    top_ref,
    total_ref,
    accum_ref,
    masks,
    load_sems,
    z_sems,
    x_sems,
    core_sems,
    recv_sems,
):
    part = lax.axis_index("parts")
    core = lax.axis_index("shard")
    blk = lax.axis_index("blk")
    z, x = blk // ALONG_X, blk % ALONG_X
    other_x, other_core = 1 - x, 1 - core

    def at(to_core, to_z, to_x):
        return (part, to_core, to_z * ALONG_X + to_x)

    bank_rows = bank_hbm.shape[0] // PIECES

    def copy(of_z, of_core, of_x, piece, sems, target):
        slot = held.at[of_z, of_core, of_x, piece]
        return pltpu.make_async_remote_copy(
            src_ref=slot,
            dst_ref=slot,
            send_sem=sems.at[of_z, of_x, piece],
            recv_sem=recv_sems.at[of_z, of_core, of_x, piece],
            device_id=target,
            device_id_type=MESH,
        )

    def along(of_z, piece, step):
        sems = z_sems.at[0 if step > 0 else 1]
        return copy(of_z, core, x, piece, sems, at(core, z + step, x))

    def across(of_z, piece):
        return copy(of_z, core, x, piece, x_sems, at(core, z, other_x))

    def over(of_z, of_x, piece):
        return copy(of_z, core, of_x, piece, core_sems, at(other_core, z, x))

    def arrived(of_z, of_core, of_x, piece):
        copy(of_z, of_core, of_x, piece, x_sems, at(core, z, other_x)).wait_recv()

    loads = [
        pltpu.make_async_copy(weight_hbm, weight_ref, load_sems.at[0]),
        pltpu.make_async_copy(queries_hbm, queries_ref, load_sems.at[1]),
    ] + [
        pltpu.make_async_copy(
            bank_hbm.at[pl.ds(piece * bank_rows, bank_rows)],
            held.at[z, core, x, piece],
            load_sems.at[2 + piece],
        )
        for piece in range(PIECES)
    ]
    for load in loads[2:]:
        load.start()

    barrier = pltpu.get_barrier_semaphore()
    below, above = z > 0, z < depth - 1

    def greet(target):
        pl.semaphore_signal(barrier, inc=1, device_id=target, device_id_type=MESH)

    greet(at(core, z, other_x))
    greet(at(other_core, z, x))
    pl.when(below)(lambda: greet(at(core, z - 1, x)))
    pl.when(above)(lambda: greet(at(core, z + 1, x)))
    pl.semaphore_wait(barrier, 2 + below.astype(jnp.int32) + above.astype(jnp.int32))

    for load in loads[2:]:
        load.wait()
    for piece in range(PIECES):
        pl.when(below)(lambda piece=piece: along(z, piece, -1).start())
        pl.when(above)(lambda piece=piece: along(z, piece, 1).start())
        across(z, piece).start()
    for piece in range(PIECES):
        over(z, x, piece).start()
    for load in loads[:2]:
        load.start()

    for load in loads[:2]:
        load.wait()
    for head in range(0, HEADS, 2):
        columns = slice(head * HEAD_DIM, (head + 2) * HEAD_DIM)
        projected[:, columns] = jnp.dot(
            queries_ref[...], weight_ref[:, columns], preferred_element_type=jnp.float32
        ).astype(jnp.bfloat16)
    for shard in range(2):
        listed = uses_ref[shard : shard + 1, :].astype(jnp.float32)
        masks[shard] = jnp.broadcast_to(listed, (HEAD_DIM, listed.shape[1])).T

    factor = HEAD_DIM**-0.5 * math.log2(math.e)
    rows = bank_hbm.shape[0]
    plane_rows = 2 * ALONG_X * rows
    rows_q = projected.shape[0]

    def attend(of_z, first):
        repeats = ALONG_X * rows // HEAD_DIM
        allowed = jnp.concatenate([masks[0]] * repeats + [masks[1]] * repeats, axis=1) > 0.5
        for head in range(HEADS):
            columns = slice(head * HEAD_DIM, (head + 1) * HEAD_DIM)
            keys = held[of_z, :, :, :, :, columns].reshape(plane_rows, HEAD_DIM)
            scores = lax.dot_general(
                projected[:, columns],
                keys,
                (((1,), (1,)), ((), ())),
                preferred_element_type=jnp.float32,
            )
            scores = jnp.where(allowed, scores * factor, NEGATIVE)
            top = jnp.max(scores, axis=1, keepdims=True)
            if not first:
                top_old = top_ref[head]
                top = jnp.maximum(top_old, top)
            weights = jnp.exp2(scores - top[:, :1])
            total = weights[:, :HEAD_DIM]
            for start in range(HEAD_DIM, plane_rows, HEAD_DIM):
                total = total + weights[:, start : start + HEAD_DIM]
            summed = jnp.dot(
                weights.astype(jnp.bfloat16), keys, preferred_element_type=jnp.float32
            )
            if first:
                top = jnp.broadcast_to(top, (rows_q, HEAD_DIM))
            else:
                shrink = jnp.exp2(top_old - top)
                total = total + total_ref[head] * shrink
                summed = summed + accum_ref[head] * shrink
            top_ref[head] = top
            total_ref[head] = total
            accum_ref[head] = summed

    def planes(distance, action):
        if distance == 0:
            action(z, 0)
            return
        pl.when(z >= distance)(lambda: action(z - distance, 1))
        pl.when(z < depth - distance)(lambda: action(z + distance, -1))

    def relay(of_z, step):
        for piece in range(PIECES):
            arrived(of_z, core, x, piece)
            pl.when((z + step >= 0) & (z + step < depth))(
                lambda piece=piece: along(of_z, piece, step).start()
            )
            across(of_z, piece).start()
            over(of_z, x, piece).start()

    def hand_over(of_z, step):
        for piece in range(PIECES):
            arrived(of_z, core, other_x, piece)
            over(of_z, other_x, piece).start()

    def finish_plane(of_z, step):
        for of_x in range(ALONG_X):
            for piece in range(PIECES):
                arrived(of_z, other_core, of_x, piece)
        attend(of_z, step == 0)

    for distance in range(depth):
        if distance + 1 < depth:
            planes(distance + 1, relay)
        planes(distance, hand_over)
        planes(distance, finish_plane)

    for head in range(HEADS):
        columns = slice(head * HEAD_DIM, (head + 1) * HEAD_DIM)
        total = jnp.sum(total_ref[head], axis=1, keepdims=True)
        out_ref[:, columns] = (accum_ref[head] / total).astype(out_ref.dtype)

    def drain(of_z, piece):
        pl.when((z >= of_z) & above)(lambda: along(of_z, piece, 1).wait_send())
        pl.when((z <= of_z) & below)(lambda: along(of_z, piece, -1).wait_send())
        across(of_z, piece).wait_send()
        for of_x in range(ALONG_X):
            over(of_z, of_x, piece).wait_send()

    for of_z in range(depth):
        for piece in range(PIECES):
            drain(of_z, piece)


def local_kernel(depth, queries_in, query_weight, bank, uses):
    rows_q, width = queries_in.shape
    rows = bank.shape[0]
    any_space = pl.BlockSpec(memory_space=pltpu.HBM)
    return pl.pallas_call(
        functools.partial(kernel, depth),
        out_shape=jax.ShapeDtypeStruct((rows_q, HEADS * HEAD_DIM), jnp.bfloat16),
        in_specs=[any_space, any_space, any_space, pl.BlockSpec(memory_space=pltpu.VMEM)],
        out_specs=pl.BlockSpec(memory_space=pltpu.VMEM),
        scratch_shapes=[
            pltpu.VMEM((depth, 2, ALONG_X, PIECES, rows // PIECES, width), jnp.bfloat16),
            pltpu.VMEM((rows_q, width), jnp.bfloat16),
            pltpu.VMEM((width, width), jnp.bfloat16),
            pltpu.VMEM((rows_q, width), jnp.bfloat16),
            pltpu.VMEM((HEADS, rows_q, HEAD_DIM), jnp.float32),
            pltpu.VMEM((HEADS, rows_q, HEAD_DIM), jnp.float32),
            pltpu.VMEM((HEADS, rows_q, HEAD_DIM), jnp.float32),
            pltpu.VMEM((2, rows_q, HEAD_DIM), jnp.float32),
            pltpu.SemaphoreType.DMA((2 + PIECES,)),
            pltpu.SemaphoreType.DMA((2, depth, ALONG_X, PIECES)),
            pltpu.SemaphoreType.DMA((depth, ALONG_X, PIECES)),
            pltpu.SemaphoreType.DMA((depth, ALONG_X, PIECES)),
            pltpu.SemaphoreType.DMA((depth, 2, ALONG_X, PIECES)),
        ],
        compiler_params=pltpu.CompilerParams(
            collective_id=0, has_side_effects=True, vmem_limit_bytes=56 * 2**20
        ),
        name="gather_attend",
    )(queries_in, query_weight, bank, uses.T)


def local_xla(queries_in, query_weight, bank, uses):
    rows = queries_in.shape[0]
    projected = jnp.dot(queries_in, query_weight, preferred_element_type=jnp.float32).astype(
        jnp.bfloat16
    )
    heads = projected.reshape(rows, HEADS, HEAD_DIM)
    whole = lax.all_gather(bank, ("shard", "blk"), axis=0, tiled=True)
    shard_rows = whole.shape[0] // 2
    chunk_rows = math.gcd(shard_rows, 512)
    chunks = shard_rows // chunk_rows
    blocked = whole.reshape(2, chunks, chunk_rows, HEADS, HEAD_DIM)
    allowed = uses > 0

    def step(carry, keys):
        top_old, total_old, accum_old = carry
        scores = jnp.einsum("thd,srhd->htsr", heads, keys, preferred_element_type=jnp.float32)
        scores = jnp.where(allowed[None, :, :, None], scores * HEAD_DIM**-0.5, NEGATIVE)
        top = jnp.maximum(top_old, jnp.max(scores, axis=(2, 3)))
        weights = jnp.exp(scores - top[:, :, None, None])
        factor = jnp.exp(top_old - top)
        total = total_old * factor + jnp.sum(weights, axis=(2, 3))
        accum = accum_old * factor[..., None] + jnp.einsum(
            "htsr,srhd->htd",
            weights.astype(jnp.bfloat16),
            keys,
            preferred_element_type=jnp.float32,
        )
        return (top, total, accum), None

    start = (
        jnp.full((HEADS, rows), NEGATIVE, jnp.float32),
        jnp.zeros((HEADS, rows), jnp.float32),
        jnp.zeros((HEADS, rows, HEAD_DIM), jnp.float32),
    )
    (top, total, accum), _ = lax.scan(step, start, blocked.transpose(1, 0, 2, 3, 4))
    out = (accum / total[..., None]).astype(jnp.bfloat16)
    return out.transpose(1, 0, 2).reshape(rows, HEADS * HEAD_DIM)


def solution(mesh):
    spec = P(("parts", "shard", "blk"), None)
    blocks = mesh.shape["blk"]
    local = functools.partial(local_kernel, blocks // ALONG_X) if blocks == 8 else local_xla
    return jax.shard_map(
        local, mesh=mesh, in_specs=(spec, P(), spec, spec), out_specs=spec, check_vma=False
    )
```

```python
import functools
import math

import jax
import jax.numpy as jnp
from jax import lax
from jax.experimental import pallas as pl
from jax.experimental.pallas import tpu as pltpu
from jax.sharding import PartitionSpec as P

HEADS = 8
HEAD_DIM = 128
NEGATIVE = -1e30
ALONG_X = 2
PIECES = 2
MESH = pl.DeviceIdType.MESH


def kernel(
    depth,
    queries_hbm,
    weight_hbm,
    bank_hbm,
    uses_ref,
    out_ref,
    held,
    queries_ref,
    weight_ref,
    projected,
    top_ref,
    total_ref,
    accum_ref,
    masks,
    load_sems,
    z_sems,
    x_sems,
    core_sems,
    recv_sems,
):
    part = lax.axis_index("parts")
    core = lax.axis_index("shard")
    blk = lax.axis_index("blk")
    z, x = blk // ALONG_X, blk % ALONG_X
    other_x, other_core = 1 - x, 1 - core

    def at(to_core, to_z, to_x):
        return (part, to_core, to_z * ALONG_X + to_x)

    bank_rows = bank_hbm.shape[0] // PIECES

    def copy(of_z, of_core, of_x, piece, sems, target):
        slot = held.at[of_z, of_core, of_x, piece]
        return pltpu.make_async_remote_copy(
            src_ref=slot,
            dst_ref=slot,
            send_sem=sems.at[of_z, of_x, piece],
            recv_sem=recv_sems.at[of_z, of_core, of_x, piece],
            device_id=target,
            device_id_type=MESH,
        )

    def along(of_z, piece, step):
        sems = z_sems.at[0 if step > 0 else 1]
        return copy(of_z, core, x, piece, sems, at(core, z + step, x))

    def across(of_z, piece):
        return copy(of_z, core, x, piece, x_sems, at(core, z, other_x))

    def over(of_z, of_x, piece):
        return copy(of_z, core, of_x, piece, core_sems, at(other_core, z, x))

    def arrived(of_z, of_core, of_x, piece):
        copy(of_z, of_core, of_x, piece, x_sems, at(core, z, other_x)).wait_recv()

    loads = [
        pltpu.make_async_copy(weight_hbm, weight_ref, load_sems.at[0]),
        pltpu.make_async_copy(queries_hbm, queries_ref, load_sems.at[1]),
    ] + [
        pltpu.make_async_copy(
            bank_hbm.at[pl.ds(piece * bank_rows, bank_rows)],
            held.at[z, core, x, piece],
            load_sems.at[2 + piece],
        )
        for piece in range(PIECES)
    ]
    for load in loads[2:]:
        load.start()

    barrier = pltpu.get_barrier_semaphore()
    below, above = z > 0, z < depth - 1

    def greet(target):
        pl.semaphore_signal(barrier, inc=1, device_id=target, device_id_type=MESH)

    greet(at(core, z, other_x))
    greet(at(other_core, z, x))
    pl.when(below)(lambda: greet(at(core, z - 1, x)))
    pl.when(above)(lambda: greet(at(core, z + 1, x)))
    pl.semaphore_wait(barrier, 2 + below.astype(jnp.int32) + above.astype(jnp.int32))

    for load in loads[2:]:
        load.wait()
    for piece in range(PIECES):
        pl.when(below)(lambda piece=piece: along(z, piece, -1).start())
        pl.when(above)(lambda piece=piece: along(z, piece, 1).start())
    for piece in range(PIECES):
        across(z, piece).start()
    for piece in range(PIECES):
        over(z, x, piece).start()
    for load in loads[:2]:
        load.start()

    factor = HEAD_DIM**-0.5 * math.log2(math.e)
    rows = bank_hbm.shape[0]
    plane_rows = 2 * ALONG_X * rows
    rows_q = projected.shape[0]

    def attend(of_z, first):
        repeats = ALONG_X * rows // HEAD_DIM
        allowed = jnp.concatenate([masks[0]] * repeats + [masks[1]] * repeats, axis=1) > 0.5
        for head in range(HEADS):
            columns = slice(head * HEAD_DIM, (head + 1) * HEAD_DIM)
            keys = held[of_z, :, :, :, :, columns].reshape(plane_rows, HEAD_DIM)
            scores = lax.dot_general(
                projected[:, columns],
                keys,
                (((1,), (1,)), ((), ())),
                preferred_element_type=jnp.float32,
            )
            scores = jnp.where(allowed, scores * factor, NEGATIVE)
            top = jnp.max(scores, axis=1, keepdims=True)
            if not first:
                top_old = top_ref[head]
                top = jnp.maximum(top_old, top)
            weights = jnp.exp2(scores - top[:, :1])
            total = weights[:, :HEAD_DIM]
            for start in range(HEAD_DIM, plane_rows, HEAD_DIM):
                total = total + weights[:, start : start + HEAD_DIM]
            summed = jnp.dot(
                weights.astype(jnp.bfloat16), keys, preferred_element_type=jnp.float32
            )
            if first:
                top = jnp.broadcast_to(top, (rows_q, HEAD_DIM))
            else:
                shrink = jnp.exp2(top_old - top)
                total = total + total_ref[head] * shrink
                summed = summed + accum_ref[head] * shrink
            top_ref[head] = top
            total_ref[head] = total
            accum_ref[head] = summed

    def project():
        for load in loads[:2]:
            load.wait()
        for head in range(0, HEADS, 2):
            columns = slice(head * HEAD_DIM, (head + 2) * HEAD_DIM)
            projected[:, columns] = jnp.dot(
                queries_ref[...], weight_ref[:, columns], preferred_element_type=jnp.float32
            ).astype(jnp.bfloat16)
        for shard in range(2):
            listed = uses_ref[shard : shard + 1, :].astype(jnp.float32)
            masks[shard] = jnp.broadcast_to(listed, (HEAD_DIM, listed.shape[1])).T

    def planes(distance, action):
        if distance == 0:
            action(z, 0)
            return
        pl.when(z >= distance)(lambda: action(z - distance, 1))
        pl.when(z < depth - distance)(lambda: action(z + distance, -1))

    def relay(of_z, step):
        for piece in range(PIECES):
            arrived(of_z, core, x, piece)
            pl.when((z + step >= 0) & (z + step < depth))(
                lambda piece=piece: along(of_z, piece, step).start()
            )
            across(of_z, piece).start()
            over(of_z, x, piece).start()

    def hand_over(of_z, step):
        for piece in range(PIECES):
            arrived(of_z, core, other_x, piece)
            over(of_z, other_x, piece).start()

    def finish_plane(of_z, step):
        for of_x in range(ALONG_X):
            for piece in range(PIECES):
                arrived(of_z, other_core, of_x, piece)
        attend(of_z, step == 0)

    for distance in range(depth):
        if distance + 1 < depth:
            planes(distance + 1, relay)
        planes(distance, hand_over)
        if distance == 0:
            project()
        planes(distance, finish_plane)

    for head in range(HEADS):
        columns = slice(head * HEAD_DIM, (head + 1) * HEAD_DIM)
        total = jnp.sum(total_ref[head], axis=1, keepdims=True)
        out_ref[:, columns] = (accum_ref[head] / total).astype(out_ref.dtype)

    def drain(of_z, piece):
        pl.when((z >= of_z) & above)(lambda: along(of_z, piece, 1).wait_send())
        pl.when((z <= of_z) & below)(lambda: along(of_z, piece, -1).wait_send())
        across(of_z, piece).wait_send()
        for of_x in range(ALONG_X):
            over(of_z, of_x, piece).wait_send()

    for of_z in range(depth):
        for piece in range(PIECES):
            drain(of_z, piece)


def local_kernel(depth, queries_in, query_weight, bank, uses):
    rows_q, width = queries_in.shape
    rows = bank.shape[0]
    any_space = pl.BlockSpec(memory_space=pltpu.HBM)
    return pl.pallas_call(
        functools.partial(kernel, depth),
        out_shape=jax.ShapeDtypeStruct((rows_q, HEADS * HEAD_DIM), jnp.bfloat16),
        in_specs=[any_space, any_space, any_space, pl.BlockSpec(memory_space=pltpu.VMEM)],
        out_specs=pl.BlockSpec(memory_space=pltpu.VMEM),
        scratch_shapes=[
            pltpu.VMEM((depth, 2, ALONG_X, PIECES, rows // PIECES, width), jnp.bfloat16),
            pltpu.VMEM((rows_q, width), jnp.bfloat16),
            pltpu.VMEM((width, width), jnp.bfloat16),
            pltpu.VMEM((rows_q, width), jnp.bfloat16),
            pltpu.VMEM((HEADS, rows_q, HEAD_DIM), jnp.float32),
            pltpu.VMEM((HEADS, rows_q, HEAD_DIM), jnp.float32),
            pltpu.VMEM((HEADS, rows_q, HEAD_DIM), jnp.float32),
            pltpu.VMEM((2, rows_q, HEAD_DIM), jnp.float32),
            pltpu.SemaphoreType.DMA((2 + PIECES,)),
            pltpu.SemaphoreType.DMA((2, depth, ALONG_X, PIECES)),
            pltpu.SemaphoreType.DMA((depth, ALONG_X, PIECES)),
            pltpu.SemaphoreType.DMA((depth, ALONG_X, PIECES)),
            pltpu.SemaphoreType.DMA((depth, 2, ALONG_X, PIECES)),
        ],
        compiler_params=pltpu.CompilerParams(
            collective_id=0, has_side_effects=True, vmem_limit_bytes=56 * 2**20
        ),
        name="gather_attend",
    )(queries_in, query_weight, bank, uses.T)


def local_xla(queries_in, query_weight, bank, uses):
    rows = queries_in.shape[0]
    projected = jnp.dot(queries_in, query_weight, preferred_element_type=jnp.float32).astype(
        jnp.bfloat16
    )
    heads = projected.reshape(rows, HEADS, HEAD_DIM)
    whole = lax.all_gather(bank, ("shard", "blk"), axis=0, tiled=True)
    shard_rows = whole.shape[0] // 2
    chunk_rows = math.gcd(shard_rows, 512)
    chunks = shard_rows // chunk_rows
    blocked = whole.reshape(2, chunks, chunk_rows, HEADS, HEAD_DIM)
    allowed = uses > 0

    def step(carry, keys):
        top_old, total_old, accum_old = carry
        scores = jnp.einsum("thd,srhd->htsr", heads, keys, preferred_element_type=jnp.float32)
        scores = jnp.where(allowed[None, :, :, None], scores * HEAD_DIM**-0.5, NEGATIVE)
        top = jnp.maximum(top_old, jnp.max(scores, axis=(2, 3)))
        weights = jnp.exp(scores - top[:, :, None, None])
        factor = jnp.exp(top_old - top)
        total = total_old * factor + jnp.sum(weights, axis=(2, 3))
        accum = accum_old * factor[..., None] + jnp.einsum(
            "htsr,srhd->htd",
            weights.astype(jnp.bfloat16),
            keys,
            preferred_element_type=jnp.float32,
        )
        return (top, total, accum), None

    start = (
        jnp.full((HEADS, rows), NEGATIVE, jnp.float32),
        jnp.zeros((HEADS, rows), jnp.float32),
        jnp.zeros((HEADS, rows, HEAD_DIM), jnp.float32),
    )
    (top, total, accum), _ = lax.scan(step, start, blocked.transpose(1, 0, 2, 3, 4))
    out = (accum / total[..., None]).astype(jnp.bfloat16)
    return out.transpose(1, 0, 2).reshape(rows, HEADS * HEAD_DIM)


def solution(mesh):
    spec = P(("parts", "shard", "blk"), None)
    blocks = mesh.shape["blk"]
    local = functools.partial(local_kernel, blocks // ALONG_X) if blocks == 8 else local_xla
    return jax.shard_map(
        local, mesh=mesh, in_specs=(spec, P(), spec, spec), out_specs=spec, check_vma=False
    )
```
